128 devices in a mesh: ij: 8 (over z, core), ab: 16 (over y, x).
Axes of the slice: x: 4, y: 4, z: 4, core: 2. Of those that a mesh axis runs over, the one named last changes fastest.
Arguments:
- amplitudes: float32 [1024, 65536], P('ab', 'ij'), may hold values from -6 to 6
- integrals: float32 [4096, 65536], P('ab', 'ij'), may hold values from -0.03125 to 0.03125
Outputs:
- residual: float32 [1024, 4096], P('ij', 'ab')
The draws below stay inside these ranges and needn't reach their ends.
All inputs are finite; a program needn't handle non-finite values.
Results may differ from the reference program's by a relative error of at most 0.000098.
Values sent between devices are 32-bit elements; how exact they have to be, the bound alone decides.
A program may use at most 128 MiB of HBM per device.

```python
import jax
import jax.numpy as jnp
from jax import lax

AB = 4096
CD = 65536
IJ = 1024


def strengthened(array, rng, source, target, blocks, factor):
    def block_of(position):
        return (jnp.arange(array.shape[position]) // (array.shape[position] // blocks)).reshape((-1,) + (1,) * (array.ndim - 1 - position))

    near = jax.random.permutation(rng, blocks)[block_of(target)]
    far = (block_of(target) + blocks // 2) % blocks
    return jnp.where((block_of(source) == near) | (block_of(source) == far), factor * array, array)


def block_scale(key, dims, cuts, low, high):
    def one(axis_at, blocks):
        draws = jax.random.uniform(jax.random.fold_in(jax.random.fold_in(key, 6), axis_at), (blocks,), jnp.float32, low / len(cuts), high / len(cuts))
        return jnp.repeat(jnp.exp(draws), dims[axis_at] // blocks).reshape((-1,) + (1,) * (len(dims) - axis_at - 1))

    level = one(*cuts[0])
    for cut in cuts[1:]:
        level = level * one(*cut)
    return level


def normal_values(key, dims, scale, most, split=(), kind=jnp.bfloat16):
    gain = block_scale(key, dims, split, -0.22, 0.18) if split else 1.0
    result = jax.random.normal(key, dims, jnp.float32) * scale * gain
    return jnp.minimum(jnp.maximum(result, -most), most).astype(kind)


def gaussian_with(own_key, extent, spread, bound, split, heavy, kind=jnp.bfloat16):
    values = spread * jax.random.normal(own_key, extent, jnp.float32)
    if split:
        values = values * block_scale(own_key, extent, split, -0.22, 0.18)
    return jnp.clip(strengthened(values, jax.random.fold_in(own_key, 3), *heavy), -bound, bound).astype(kind)


def setup_inputs(seed: int = 0) -> dict:
    keys = jax.random.split(jax.random.key(seed), 3)
    return {
        "amplitudes": normal_values(keys[0], (IJ, CD), 1.0, 6.0, ((0, 16), (1, 8)), jnp.float32),
        "integrals": gaussian_with(keys[1], (AB, CD), CD ** -0.5, 0.03125, ((0, 16), (1, 8)), (1, 0, 16, 2.0), jnp.float32),
    }


def reference(amplitudes, integrals):
    return lax.dot_general(amplitudes, integrals, (((1,), (1,)), ((), ())), precision=lax.Precision.HIGHEST, preferred_element_type=jnp.float32)
```

```python
import functools

import jax
import jax.numpy as jnp
from jax import lax
from jax.experimental import pallas as pl
from jax.experimental.pallas import tpu as pltpu
from jax.sharding import PartitionSpec as P

SIDE = 4
KQ = 2048
TROWS = 64
VROWS = 256
MZ = 256
CHUNKS = (64, 64, 64, 64)
VMEM_BYTES = 60 << 20


def place():
    ij, ab = lax.axis_index("ij"), lax.axis_index("ab")
    return ab % SIDE, ab // SIDE, ij // 2, ij % 2


def dot_nt(left, right):
    return lax.dot_general(left, right, (((1,), (1,)), ((), ())), preferred_element_type=jnp.float32)


def split(value):
    high = value.astype(jnp.bfloat16)
    return high, (value - high.astype(jnp.float32)).astype(jnp.bfloat16)


def kernel(t_ref, v_ref, o_ref, tbuf, vbuf, thi, tlo, vhi, vlo, ct, zbuf, zs, abuf, asum, cbuf,
           t_send, t_recv, g_send, g_recv, f_send, f_recv, v_send, v_recv, z_send, z_recv, a_send, a_recv,
           c_send, c_recv, local_sem):
    x, y, z, c = place()
    a = x * (1 - c) + y * c
    b = y * (1 - c) + x * c

    def device(a_to, b_to, z_to, c_to):
        x_to = a_to * (1 - c) + b_to * c
        y_to = b_to * (1 - c) + a_to * c
        return (z_to * 2 + c_to, y_to * SIDE + x_to)

    def slot(b_of, a_of):
        return (b_of * (1 - c) + a_of * c) * SIDE + a_of * (1 - c) + b_of * c

    def shifted(position, by):
        return (position + by + SIDE) % SIDE

    def along_a(by):
        return device(shifted(a, by), b, z, c)

    def along_b(by):
        return device(a, shifted(b, by), z, c)

    def along_z(by):
        return device(a, b, shifted(z, by), c)

    other_core = (z * 2 + 1 - c, y * SIDE + x)

    def columns(of):
        return pl.ds(pl.multiple_of(of * KQ, KQ), KQ)

    def remote(src, dst, send, recv, to):
        return pltpu.make_async_remote_copy(src_ref=src, dst_ref=dst, send_sem=send, recv_sem=recv, device_id=to,
                                            device_id_type=pl.DeviceIdType.MESH)

    barrier = pltpu.get_barrier_semaphore()
    peers = [along_a(j) for j in (1, 2, 3)] + [along_b(1), along_b(-1)] + [along_z(j) for j in (1, 2, 3)] + [other_core]
    for peer in peers:
        pl.semaphore_signal(barrier, inc=1, device_id=peer, device_id_type=pl.DeviceIdType.MESH)
    pl.semaphore_wait(barrier, len(peers))

    sent = []

    def go(copy):
        copy.start()
        sent.append(copy)
        return copy

    t_copies = {}
    for j in (1, 3, 2):
        t_copies[j] = go(remote(t_ref.at[:, columns(shifted(a, j))], tbuf.at[slot(b, a)], t_send.at[j], t_recv.at[j], along_a(j)))
    t_own = pltpu.make_async_copy(t_ref.at[:, columns(a)], tbuf.at[slot(b, a)], local_sem.at[0])
    t_own.start()
    v_own = pltpu.make_async_copy(v_ref.at[:, columns(a)], vbuf.at[a], local_sem.at[1])
    v_own.start()

    g_copies, f_copies = {}, {}

    def gather(j, src):
        dst = tbuf.at[slot(b, shifted(a, -j))]
        g_copies[j] = [go(remote(src, dst, g_send.at[2 * j + w], g_recv.at[2 * j + w], along_b(by))) for w, by in ((0, 1), (1, -1))]

    def forward(j):
        a_of = shifted(a, -j)
        f_copies[j] = []
        for w, by in ((0, 1), (1, -1)):
            g_copies[j][w].wait_recv()
            part = tbuf.at[slot(shifted(b, -by), a_of), pl.ds(w * (TROWS // 2), TROWS // 2)]
            f_copies[j].append(go(remote(part, part, f_send.at[2 * j + w], f_recv.at[2 * j + w], along_b(by))))

    v_copies = {}
    starts = [sum(CHUNKS[:k]) for k in range(len(CHUNKS))]

    def send_v(k):
        rows = pl.ds(starts[k], CHUNKS[k])
        v_copies[k] = [go(remote(v_ref.at[rows, columns(shifted(a, j))], vbuf.at[a, rows], v_send.at[3 * k + j - 1],
                                 v_recv.at[3 * k + j - 1], along_a(j))) for j in (1, 3, 2)]

    def convert_t(b_of, a_of):
        s = slot(b_of, a_of)
        rows = pl.ds(pl.multiple_of(s * TROWS, TROWS), TROWS)
        thi[rows, :], tlo[rows, :] = split(tbuf[s])

    gather(0, t_ref.at[:, columns(a)])
    send_v(0)
    t_copies[1].wait_recv()
    gather(1, tbuf.at[slot(b, shifted(a, -1))])
    t_copies[3].wait_recv()
    gather(3, tbuf.at[slot(b, shifted(a, -3))])
    forward(0)
    t_copies[2].wait_recv()
    gather(2, tbuf.at[slot(b, shifted(a, -2))])
    t_own.wait()
    convert_t(b, a)
    for j in (1, 3, 2):
        convert_t(b, shifted(a, -j))
    for j in (1, 3, 2):
        forward(j)
    send_v(1)
    for j in (0, 1, 3, 2):
        for by in (1, -1):
            convert_t(shifted(b, -by), shifted(a, -j))
    for j in (0, 1, 3, 2):
        for copy in f_copies[j]:
            copy.wait_recv()
        convert_t(shifted(b, 2), shifted(a, -j))
    v_own.wait()

    z_copies, a_copies, c_copies = {}, {}, {}

    def lanes_of(z_of):
        return pl.ds(pl.multiple_of(z_of * MZ, MZ), MZ)

    def multiply(k):
        size = CHUNKS[k]
        for copy in v_copies[k]:
            copy.wait_recv()
        for s in range(SIDE):
            rows = pl.ds(s * size, size)
            vhi[rows, :], vlo[rows, :] = split(vbuf[s, pl.ds(starts[k], size), :])
        n = pl.ds(0, SIDE * size)
        z_copies[k] = []
        for j in (1, 2, 3, 0):
            m = lanes_of(shifted(z, j))
            ct[k, n, m] = dot_nt(vhi[n, :], thi[m, :]) + dot_nt(vhi[n, :], tlo[m, :]) + dot_nt(vlo[n, :], thi[m, :])
            if j:
                z_copies[k].append(go(remote(ct.at[k, n, m], zbuf.at[k, j - 1, n], z_send.at[3 * k + j - 1],
                                             z_recv.at[3 * k + j - 1], along_z(j))))

    def reduce_z(k):
        size = CHUNKS[k]
        n = pl.ds(0, SIDE * size)
        for copy in z_copies[k]:
            copy.wait_recv()
        zs[k, n, :] = ct[k, n, lanes_of(z)] + zbuf[k, 0, n, :] + zbuf[k, 1, n, :] + zbuf[k, 2, n, :]
        a_copies[k] = []
        for j in (1, 3, 2):
            part = pl.ds(pl.multiple_of(shifted(a, j) * size, size), size)
            a_copies[k].append(go(remote(zs.at[k, part], abuf.at[k, j - 1, pl.ds(0, size)], a_send.at[3 * k + j - 1],
                                         a_recv.at[3 * k + j - 1], along_a(j))))

    def half(core):
        return pl.ds(pl.multiple_of(core * (MZ // 2), MZ // 2), MZ // 2)

    def reduce_a(k):
        size = CHUNKS[k]
        for copy in a_copies[k]:
            copy.wait_recv()
        own = zs[k, pl.ds(pl.multiple_of(a * size, size), size), :]
        rows = pl.ds(starts[k], size)
        q = pl.ds(0, size)
        asum[rows, :] = own + abuf[k, 0, q, :] + abuf[k, 1, q, :] + abuf[k, 2, q, :]
        c_copies[k] = go(remote(asum.at[rows, half(1 - c)], cbuf.at[rows], c_send.at[k], c_recv.at[k], other_core))

    def finish(k):
        c_copies[k].wait_recv()

    last = len(CHUNKS)
    for k in range(last + 3):
        if k < last:
            if k + 2 < last:
                send_v(k + 2)
            multiply(k)
        if 1 <= k <= last:
            reduce_z(k - 1)
        if 2 <= k <= last + 1:
            reduce_a(k - 2)
        if 3 <= k:
            finish(k - 3)
    o_ref[...] = (asum[:, half(c)] + cbuf[...]).T
    for copy in sent:
        copy.wait_send()


def local(amplitudes, integrals):
    steps, most = len(CHUNKS), max(CHUNKS)
    bf16, f32 = jnp.bfloat16, jnp.float32
    dma = pltpu.SemaphoreType.DMA
    return pl.pallas_call(
        kernel,
        out_shape=jax.ShapeDtypeStruct((MZ // 2, VROWS), f32),
        in_specs=[pl.BlockSpec(memory_space=pl.ANY)] * 2,
        out_specs=pl.BlockSpec(memory_space=pltpu.VMEM),
        scratch_shapes=[
            pltpu.VMEM((SIDE * SIDE, TROWS, KQ), f32),
            pltpu.VMEM((SIDE, VROWS, KQ), f32),
            pltpu.VMEM((SIDE * SIDE * TROWS, KQ), bf16),
            pltpu.VMEM((SIDE * SIDE * TROWS, KQ), bf16),
            pltpu.VMEM((SIDE * most, KQ), bf16),
            pltpu.VMEM((SIDE * most, KQ), bf16),
            pltpu.VMEM((steps, SIDE * most, SIDE * MZ), f32),
            pltpu.VMEM((steps, SIDE - 1, SIDE * most, MZ), f32),
            pltpu.VMEM((steps, SIDE * most, MZ), f32),
            pltpu.VMEM((steps, SIDE - 1, most, MZ), f32),
            pltpu.VMEM((VROWS, MZ), f32),
            pltpu.VMEM((VROWS, MZ // 2), f32),
            dma((SIDE,)), dma((SIDE,)),
            dma((2 * SIDE,)), dma((2 * SIDE,)),
            dma((2 * SIDE,)), dma((2 * SIDE,)),
            dma((3 * steps,)), dma((3 * steps,)),
            dma((3 * steps,)), dma((3 * steps,)),
            dma((3 * steps,)), dma((3 * steps,)),
            dma((steps,)), dma((steps,)),
            dma((2,)),
        ],
        compiler_params=pltpu.CompilerParams(collective_id=0, has_side_effects=True, vmem_limit_bytes=VMEM_BYTES),
        cost_estimate=pl.CostEstimate(flops=3 * 2 * 1024 * 1024 * KQ, bytes_accessed=10 << 20, transcendentals=0),
    )(amplitudes, integrals)


def solution(mesh):
    in_specs = (P("ab", "ij"), P("ab", "ij"))
    out_specs = P("ij", "ab")
    return jax.shard_map(local, mesh=mesh, in_specs=in_specs, out_specs=out_specs, check_vma=False)
```

```python
import functools

import jax
import jax.numpy as jnp
from jax import lax
from jax.experimental import pallas as pl
from jax.experimental.pallas import tpu as pltpu
from jax.sharding import PartitionSpec as P

SIDE = 4
KQ = 2048
TROWS = 64
VROWS = 256
MZ = 256
CHUNKS = (64, 64, 64, 32, 32)
A_FIRST = 2
VMEM_BYTES = 60 << 20


def place():
    ij, ab = lax.axis_index("ij"), lax.axis_index("ab")
    return ab % SIDE, ab // SIDE, ij // 2, ij % 2


def dot_nt(left, right):
    return lax.dot_general(left, right, (((1,), (1,)), ((), ())), preferred_element_type=jnp.float32)


def split(value):
    high = value.astype(jnp.bfloat16)
    return high, (value - high.astype(jnp.float32)).astype(jnp.bfloat16)


def kernel(t_ref, v_ref, o_ref, tbuf, vbuf, thi, tlo, vhl, ct, zbuf, zs, abuf, afirst, zdirect, asum, cbuf, out,
           t_send, t_recv, g_send, g_recv, f_send, f_recv, v_send, v_recv, z_send, z_recv, a_send, a_recv,
           d_send, d_recv, b_send, b_recv, c_send, c_recv, o_sem, local_sem):
    x, y, z, c = place()
    a = x * (1 - c) + y * c
    b = y * (1 - c) + x * c

    def device(a_to, b_to, z_to, c_to):
        x_to = a_to * (1 - c) + b_to * c
        y_to = b_to * (1 - c) + a_to * c
        return (z_to * 2 + c_to, y_to * SIDE + x_to)

    def slot(b_of, a_of):
        return (b_of * (1 - c) + a_of * c) * SIDE + a_of * (1 - c) + b_of * c

    def shifted(position, by):
        return (position + by + SIDE) % SIDE

    def along_a(by):
        return device(shifted(a, by), b, z, c)

    def along_b(by):
        return device(a, shifted(b, by), z, c)

    def along_z(by):
        return device(a, b, shifted(z, by), c)

    other_core = (z * 2 + 1 - c, y * SIDE + x)

    def columns(of):
        return pl.ds(pl.multiple_of(of * KQ, KQ), KQ)

    def remote(src, dst, send, recv, to):
        return pltpu.make_async_remote_copy(src_ref=src, dst_ref=dst, send_sem=send, recv_sem=recv, device_id=to,
                                            device_id_type=pl.DeviceIdType.MESH)

    barrier = pltpu.get_barrier_semaphore()
    peers = [along_a(j) for j in (1, 2, 3)] + [along_b(1), along_b(-1)] + [along_z(j) for j in (1, 2, 3)] + [other_core]
    peers += [device(a, b, shifted(z, j), 1 - c) for j in (1, 2, 3)]
    for peer in peers:
        pl.semaphore_signal(barrier, inc=1, device_id=peer, device_id_type=pl.DeviceIdType.MESH)
    pl.semaphore_wait(barrier, len(peers))

    sent = []

    def go(copy):
        copy.start()
        sent.append(copy)
        return copy

    t_copies = {}
    for j in (1, 3, 2):
        t_copies[j] = go(remote(t_ref.at[:, columns(shifted(a, j))], tbuf.at[slot(b, a)], t_send.at[j], t_recv.at[j], along_a(j)))
    t_own = pltpu.make_async_copy(t_ref.at[:, columns(a)], tbuf.at[slot(b, a)], local_sem.at[0])
    t_own.start()
    v_own = pltpu.make_async_copy(v_ref.at[:, columns(a)], vbuf.at[a], local_sem.at[1])
    v_own.start()

    g_copies = {}

    def gather(j, src):
        dst = tbuf.at[slot(b, shifted(a, -j))]
        g_copies[j] = [go(remote(src, dst, g_send.at[2 * j + w], g_recv.at[2 * j + w], along_b(by))) for w, by in ((0, 1), (1, -1))]

    def f_copy(j, w):
        by = 1 - 2 * w
        part = tbuf.at[slot(shifted(b, -by), shifted(a, -j)), pl.ds(w * (TROWS // 2), TROWS // 2)]
        return remote(part, part, f_send.at[2 * j + w], f_recv.at[2 * j + w], along_b(by))

    def forward(j):
        for w in (0, 1):
            g_copies[j][w].wait_recv()
            go(f_copy(j, w))

    v_copies = {}
    starts = [sum(CHUNKS[:k]) for k in range(len(CHUNKS))]

    def send_v(k):
        rows = pl.ds(starts[k], CHUNKS[k])
        v_copies[k] = [go(remote(v_ref.at[rows, columns(shifted(a, j))], vbuf.at[a, rows], v_send.at[3 * k + j - 1],
                                 v_recv.at[3 * k + j - 1], along_a(j))) for j in (1, 3, 2)]

    def convert_t(b_of, a_of):
        s = slot(b_of, a_of)
        rows = pl.ds(pl.multiple_of(s * TROWS, TROWS), TROWS)
        thi[rows, :], tlo[rows, :] = split(tbuf[s])

    def convert_sides(j):
        for by in (1, -1):
            convert_t(shifted(b, -by), shifted(a, -j))

    z_copies, a_copies, c_copies = {}, {}, {}

    def lanes_of(z_of):
        return pl.ds(pl.multiple_of(z_of * MZ, MZ), MZ)

    def half(core):
        return pl.ds(pl.multiple_of(core * (MZ // 2), MZ // 2), MZ // 2)

    last = len(CHUNKS)
    z_first = [k < last - A_FIRST for k in range(last)]

    def convert_v(k):
        size = CHUNKS[k]
        n = SIDE * size
        for copy in v_copies[k]:
            copy.wait_recv()

        @pl.loop(0, SIDE)
        def _(s):
            high, low = pl.ds(pl.multiple_of(s * size, size), size), pl.ds(pl.multiple_of(n + s * size, size), size)
            vhl[high, :], vhl[low, :] = split(vbuf[s, pl.ds(starts[k], size), :])

        a_copies[k] = []

    def multiply(k, m):
        n = SIDE * CHUNKS[k]
        both = dot_nt(vhl[pl.ds(0, 2 * n), :], thi[m, :])
        ct[k, pl.ds(0, n), m] = both[:n] + both[n:] + dot_nt(vhl[pl.ds(0, n), :], tlo[m, :])

    def z_copy(k, j):
        n = pl.ds(0, SIDE * CHUNKS[k])
        return remote(ct.at[k, n, lanes_of(shifted(z, j))], zbuf.at[k, j - 1, n], z_send.at[3 * k + j - 1],
                      z_recv.at[3 * k + j - 1], along_z(j))

    def wait_later(copies):
        sent.extend(copies)
        return copies

    def early_tiles():
        @pl.loop(0, SIDE)
        def _(i):
            j = i + i // 2 - 2 * (i // 3)
            for w in (0, 1):
                f_copy(j, w).wait_recv()
            convert_t(shifted(b, 2), shifted(a, -j))
            z_of = shifted(y, -j)
            multiply(0, lanes_of(z_of))
            by = shifted(z_of, -z)

            @pl.when(by != 0)
            def _():
                z_copy(0, by).start()

        z_copies[0] = wait_later([z_copy(0, j) for j in (1, 2, 3)])

    def a_first_copy(k, j, i):
        size, f = CHUNKS[k], k - last + A_FIRST
        m = lanes_of(shifted(z, j))
        part = pl.ds(pl.multiple_of(shifted(a, i) * size, size), size)
        at = 12 * f + 3 * j + i - 1
        return remote(ct.at[k, part, m], afirst.at[f, i - 1, pl.ds(0, size), m], b_send.at[at], b_recv.at[at], along_a(i))

    def all_tiles(k):
        convert_v(k)

        @pl.loop(0, SIDE)
        def _(step):
            j = (step + 1) % SIDE
            multiply(k, lanes_of(shifted(z, j)))
            if z_first[k]:
                @pl.when(step < SIDE - 1)
                def _():
                    z_copy(k, j).start()
            else:
                for i in (2, 1, 3):
                    a_first_copy(k, j, i).start()

        if z_first[k]:
            z_copies[k] = wait_later([z_copy(k, j) for j in (1, 2, 3)])
        else:
            z_copies[k] = []
            a_copies[k] = wait_later([a_first_copy(k, j, i) for j in (1, 2, 3, 0) for i in (2, 1, 3)])

    def reduce_first(k):
        size = CHUNKS[k]
        q = pl.ds(0, size)
        if z_first[k]:
            n = pl.ds(0, SIDE * size)
            for copy in z_copies[k]:
                copy.wait_recv()
            zs[k, n, :] = ct[k, n, lanes_of(z)] + zbuf[k, 0, n, :] + zbuf[k, 1, n, :] + zbuf[k, 2, n, :]
            for j in (2, 1, 3):
                part = pl.ds(pl.multiple_of(shifted(a, j) * size, size), size)
                a_copies[k].append(go(remote(zs.at[k, part], abuf.at[k, j - 1, q], a_send.at[3 * k + j - 1],
                                             a_recv.at[3 * k + j - 1], along_a(j))))
        else:
            f = k - last + A_FIRST
            own = pl.ds(pl.multiple_of(a * size, size), size)
            for i, j in enumerate((1, 2, 3, 0)):
                m = lanes_of(shifted(z, j))
                for copy in a_copies[k][3 * i : 3 * i + 3]:
                    copy.wait_recv()
                ct[k, own, m] = ct[k, own, m] + afirst[f, 0, q, m] + afirst[f, 1, q, m] + afirst[f, 2, q, m]
                for core in (0, 1):
                    if j or core:
                        at = 2 * j + core - 1
                        part = pl.ds(pl.multiple_of(shifted(z, j) * MZ + ((c + core) % 2) * (MZ // 2), MZ // 2), MZ // 2)
                        z_copies[k].append(go(remote(ct.at[k, own, part], zdirect.at[f, at, q], d_send.at[7 * f + at],
                                                     d_recv.at[7 * f + at], device(a, b, shifted(z, j), (c + core) % 2))))

    def write(k, value):
        rows = pl.ds(starts[k], CHUNKS[k])
        out[rows, :] = value
        written.append(pltpu.make_async_copy(out.at[rows], o_ref.at[rows], o_sem.at[k]))
        written[-1].start()

    written = []

    def reduce_second(k):
        size = CHUNKS[k]
        rows = pl.ds(starts[k], size)
        own = pl.ds(pl.multiple_of(a * size, size), size)
        q = pl.ds(0, size)
        if z_first[k]:
            for copy in a_copies[k]:
                copy.wait_recv()
            asum[rows, :] = zs[k, own, :] + abuf[k, 0, q, :] + abuf[k, 1, q, :] + abuf[k, 2, q, :]
            c_copies[k] = go(remote(asum.at[rows, half(1 - c)], cbuf.at[rows], c_send.at[k], c_recv.at[k], other_core))

    def finish(k):
        size = CHUNKS[k]
        rows = pl.ds(starts[k], size)
        q = pl.ds(0, size)
        if z_first[k]:
            c_copies[k].wait_recv()
            write(k, asum[rows, half(c)] + cbuf[rows, :])
        else:
            f = k - last + A_FIRST
            own = pl.ds(pl.multiple_of(a * size, size), size)
            value = ct[k, own, pl.ds(pl.multiple_of(z * MZ + c * (MZ // 2), MZ // 2), MZ // 2)]
            for copy in z_copies[k]:
                copy.wait_recv()
            for at in range(7):
                value += zdirect[f, at, q, :]
            write(k, value)

    gather(0, t_ref.at[:, columns(a)])
    send_v(0)
    t_copies[1].wait_recv()
    gather(1, tbuf.at[slot(b, shifted(a, -1))])
    t_copies[3].wait_recv()
    gather(3, tbuf.at[slot(b, shifted(a, -3))])
    forward(0)
    t_copies[2].wait_recv()
    gather(2, tbuf.at[slot(b, shifted(a, -2))])
    t_own.wait()
    v_own.wait()
    pl.loop(0, SIDE)(lambda j: convert_t(b, shifted(a, -j)))
    forward(1)
    forward(3)
    forward(2)
    send_v(1)
    pl.loop(0, SIDE)(convert_sides)
    convert_v(0)
    early_tiles()

    for k in range(1, last):
        for later in range(2 if k == 1 else k + 2, min(k + 3, last)):
            send_v(later)
        all_tiles(k)
        if 2 <= k < last - A_FIRST + 1:
            reduce_first(k - 2)
    for k in range(last - A_FIRST - 1, last):
        reduce_first(k)
    for k in range(last):
        reduce_second(k)
    for k in range(last):
        finish(k)
    for copy in sent:
        copy.wait_send()
    for copy in written:
        copy.wait()


def local(amplitudes, integrals):
    steps, most = len(CHUNKS), max(CHUNKS)
    bf16, f32 = jnp.bfloat16, jnp.float32
    dma = pltpu.SemaphoreType.DMA
    return pl.pallas_call(
        kernel,
        out_shape=jax.ShapeDtypeStruct((VROWS, MZ // 2), f32),
        in_specs=[pl.BlockSpec(memory_space=pl.ANY)] * 2,
        out_specs=pl.BlockSpec(memory_space=pl.ANY),
        scratch_shapes=[
            pltpu.VMEM((SIDE * SIDE, TROWS, KQ), f32),
            pltpu.VMEM((SIDE, VROWS, KQ), f32),
            pltpu.VMEM((SIDE * SIDE * TROWS, KQ), bf16),
            pltpu.VMEM((SIDE * SIDE * TROWS, KQ), bf16),
            pltpu.VMEM((2 * SIDE * most, KQ), bf16),
            pltpu.VMEM((steps, SIDE * most, SIDE * MZ), f32),
            pltpu.VMEM((steps, SIDE - 1, SIDE * most, MZ), f32),
            pltpu.VMEM((steps, SIDE * most, MZ), f32),
            pltpu.VMEM((steps, SIDE - 1, most, MZ), f32),
            pltpu.VMEM((A_FIRST, SIDE - 1, most, SIDE * MZ), f32),
            pltpu.VMEM((A_FIRST, 7, most, MZ // 2), f32),
            pltpu.VMEM((VROWS, MZ), f32),
            pltpu.VMEM((VROWS, MZ // 2), f32),
            pltpu.VMEM((VROWS, MZ // 2), f32),
            dma((SIDE,)), dma((SIDE,)),
            dma((2 * SIDE,)), dma((2 * SIDE,)),
            dma((2 * SIDE,)), dma((2 * SIDE,)),
            dma((3 * steps,)), dma((3 * steps,)),
            dma((3 * steps,)), dma((3 * steps,)),
            dma((3 * steps,)), dma((3 * steps,)),
            dma((7 * A_FIRST,)), dma((7 * A_FIRST,)),
            dma((12 * A_FIRST,)), dma((12 * A_FIRST,)),
            dma((steps,)), dma((steps,)),
            dma((steps,)),
            dma((2,)),
        ],
        compiler_params=pltpu.CompilerParams(collective_id=0, has_side_effects=True, vmem_limit_bytes=VMEM_BYTES),
        cost_estimate=pl.CostEstimate(flops=3 * 2 * 1024 * 1024 * KQ, bytes_accessed=10 << 20, transcendentals=0),
    )(amplitudes, integrals).T


def solution(mesh):
    in_specs = (P("ab", "ij"), P("ab", "ij"))
    out_specs = P("ij", "ab")
    return jax.shard_map(local, mesh=mesh, in_specs=in_specs, out_specs=out_specs, check_vma=False)
```

```python
import functools

import jax
import jax.numpy as jnp
from jax import lax
from jax.experimental import pallas as pl
from jax.experimental.pallas import tpu as pltpu
from jax.sharding import PartitionSpec as P

SIDE = 4
KQ = 2048
TROWS = 64
VROWS = 256
MZ = 256
CHUNKS = (64, 64, 64, 32, 32)
A_FIRST = 2
VMEM_BYTES = 60 << 20


def place():
    ij, ab = lax.axis_index("ij"), lax.axis_index("ab")
    return ab % SIDE, ab // SIDE, ij // 2, ij % 2


def dot_nt(left, right):
    return lax.dot_general(left, right, (((1,), (1,)), ((), ())), preferred_element_type=jnp.float32)


def split(value):
    high = value.astype(jnp.bfloat16)
    return high, (value - high.astype(jnp.float32)).astype(jnp.bfloat16)


def kernel(t_ref, v_ref, o_ref, tbuf, vbuf, thi, tlo, vhl, ct, zbuf, zs, abuf, afirst, zdirect, asum, cbuf,
           t_send, t_recv, g_send, g_recv, f_send, f_recv, v_send, v_recv, z_send, z_recv, a_send, a_recv,
           d_send, d_recv, b_send, b_recv, c_send, c_recv, local_sem):
    x, y, z, c = place()
    a = x * (1 - c) + y * c
    b = y * (1 - c) + x * c

    def device(a_to, b_to, z_to, c_to):
        x_to = a_to * (1 - c) + b_to * c
        y_to = b_to * (1 - c) + a_to * c
        return (z_to * 2 + c_to, y_to * SIDE + x_to)

    def slot(b_of, a_of):
        return (b_of * (1 - c) + a_of * c) * SIDE + a_of * (1 - c) + b_of * c

    def shifted(position, by):
        return (position + by + SIDE) % SIDE

    def along_a(by):
        return device(shifted(a, by), b, z, c)

    def along_b(by):
        return device(a, shifted(b, by), z, c)

    def along_z(by):
        return device(a, b, shifted(z, by), c)

    other_core = (z * 2 + 1 - c, y * SIDE + x)

    def columns(of):
        return pl.ds(pl.multiple_of(of * KQ, KQ), KQ)

    def remote(src, dst, send, recv, to):
        return pltpu.make_async_remote_copy(src_ref=src, dst_ref=dst, send_sem=send, recv_sem=recv, device_id=to,
                                            device_id_type=pl.DeviceIdType.MESH)

    barrier = pltpu.get_barrier_semaphore()
    peers = [along_a(j) for j in (1, 2, 3)] + [along_b(1), along_b(-1)] + [along_z(j) for j in (1, 2, 3)] + [other_core]
    peers += [device(a, b, shifted(z, j), 1 - c) for j in (1, 2, 3)]
    for peer in peers:
        pl.semaphore_signal(barrier, inc=1, device_id=peer, device_id_type=pl.DeviceIdType.MESH)
    pl.semaphore_wait(barrier, len(peers))

    sent = []

    def go(copy):
        copy.start()
        return copy

    def wait_sent(like, sem):
        sent.append(remote(like, like, sem, sem, other_core))

    def wait_received(like, sem):
        remote(like, like, sem, sem, other_core).wait_recv()

    t_copies = {}
    for j in (1, 3, 2):
        t_copies[j] = go(remote(t_ref.at[:, columns(shifted(a, j))], tbuf.at[slot(b, a)], t_send, t_recv.at[j - 1], along_a(j)))
    wait_sent(vbuf.at[0, pl.ds(0, 3 * TROWS)], t_send)
    t_own = pltpu.make_async_copy(t_ref.at[:, columns(a)], tbuf.at[slot(b, a)], local_sem.at[0])
    t_own.start()
    v_own = pltpu.make_async_copy(v_ref.at[:, columns(a)], vbuf.at[a], local_sem.at[1])
    v_own.start()

    g_copies = {}
    wait_sent(vbuf.at[pl.ds(0, 2)], g_send)
    wait_sent(vbuf.at[0], f_send)

    def gather(j, src):
        dst = tbuf.at[slot(b, shifted(a, -j))]
        g_copies[j] = [go(remote(src, dst, g_send, g_recv.at[2 * j + w], along_b(by))) for w, by in ((0, 1), (1, -1))]

    def f_copy(j, w):
        by = 1 - 2 * w
        part = tbuf.at[slot(shifted(b, -by), shifted(a, -j)), pl.ds(w * (TROWS // 2), TROWS // 2)]
        return remote(part, part, f_send, f_recv.at[j], along_b(by))

    def forward(j):
        for w in (0, 1):
            g_copies[j][w].wait_recv()
            go(f_copy(j, w))

    wait_sent(vbuf.at[pl.ds(0, 3)], v_send)
    starts = [sum(CHUNKS[:k]) for k in range(len(CHUNKS))]

    def send_v(k):
        rows = pl.ds(starts[k], CHUNKS[k])
        for j in (1, 3, 2):
            go(remote(v_ref.at[rows, columns(shifted(a, j))], vbuf.at[a, rows], v_send, v_recv.at[k], along_a(j)))

    def convert_t(b_of, a_of):
        s = slot(b_of, a_of)
        rows = pl.ds(pl.multiple_of(s * TROWS, TROWS), TROWS)
        thi[rows, :], tlo[rows, :] = split(tbuf[s])

    def convert_sides(j):
        for by in (1, -1):
            convert_t(shifted(b, -by), shifted(a, -j))

    c_copies = {}

    def lanes_of(z_of):
        return pl.ds(pl.multiple_of(z_of * MZ, MZ), MZ)

    def half(core):
        return pl.ds(pl.multiple_of(core * (MZ // 2), MZ // 2), MZ // 2)

    last = len(CHUNKS)
    z_first = [k < last - A_FIRST for k in range(last)]

    def convert_v(k):
        size = CHUNKS[k]
        n = SIDE * size
        wait_received(vbuf.at[pl.ds(0, 3), pl.ds(starts[k], size)], v_recv.at[k])

        @pl.loop(0, SIDE)
        def _(s):
            high, low = pl.ds(pl.multiple_of(s * size, size), size), pl.ds(pl.multiple_of(n + s * size, size), size)
            vhl[high, :], vhl[low, :] = split(vbuf[s, pl.ds(starts[k], size), :])

    def multiply(k, m):
        n = SIDE * CHUNKS[k]
        both = dot_nt(vhl[pl.ds(0, 2 * n), :], thi[m, :])
        ct[k, pl.ds(0, n), m] = both[:n] + both[n:] + dot_nt(vhl[pl.ds(0, n), :], tlo[m, :])

    def z_copy(k, j):
        n = pl.ds(0, SIDE * CHUNKS[k])
        return remote(ct.at[k, n, lanes_of(shifted(z, j))], zbuf.at[k, j - 1, n], z_send.at[k], z_recv.at[k], along_z(j))

    def early_tiles():
        @pl.loop(0, SIDE)
        def _(i):
            j = i + i // 2 - 2 * (i // 3)
            wait_received(tbuf.at[0], f_recv.at[j])
            convert_t(shifted(b, 2), shifted(a, -j))
            z_of = shifted(y, -j)
            multiply(0, lanes_of(z_of))
            by = shifted(z_of, -z)

            @pl.when(by != 0)
            def _():
                z_copy(0, by).start()

        wait_sent(zbuf.at[0, :, pl.ds(0, SIDE * CHUNKS[0])], z_send.at[0])

    def a_first_copy(k, j, i):
        size, f = CHUNKS[k], k - last + A_FIRST
        m = lanes_of(shifted(z, j))
        part = pl.ds(pl.multiple_of(shifted(a, i) * size, size), size)
        return remote(ct.at[k, part, m], afirst.at[f, i - 1, pl.ds(0, size), m], b_send.at[f],
                      b_recv.at[SIDE * f + j], along_a(i))

    def all_tiles(k):
        convert_v(k)

        @pl.loop(0, SIDE)
        def _(step):
            j = (step + 1) % SIDE
            multiply(k, lanes_of(shifted(z, j)))
            if z_first[k]:
                @pl.when(step < SIDE - 1)
                def _():
                    z_copy(k, j).start()
            else:
                for i in (2, 1, 3):
                    a_first_copy(k, j, i).start()

        if z_first[k]:
            wait_sent(zbuf.at[k, :, pl.ds(0, SIDE * CHUNKS[k])], z_send.at[k])
        else:
            f = k - last + A_FIRST
            wait_sent(afirst.at[f, :, pl.ds(0, CHUNKS[k])], b_send.at[f])

    def reduce_first(k):
        size = CHUNKS[k]
        q = pl.ds(0, size)
        if z_first[k]:
            n = pl.ds(0, SIDE * size)
            wait_received(zbuf.at[k, :, n], z_recv.at[k])
            zs[k, n, :] = ct[k, n, lanes_of(z)] + zbuf[k, 0, n, :] + zbuf[k, 1, n, :] + zbuf[k, 2, n, :]
            for j in (2, 1, 3):
                part = pl.ds(pl.multiple_of(shifted(a, j) * size, size), size)
                go(remote(zs.at[k, part], abuf.at[k, j - 1, q], a_send.at[k], a_recv.at[k], along_a(j)))
            wait_sent(abuf.at[k, :, q], a_send.at[k])
        else:
            f = k - last + A_FIRST
            own = pl.ds(pl.multiple_of(a * size, size), size)
            for j in (1, 2, 3, 0):
                m = lanes_of(shifted(z, j))
                wait_received(afirst.at[f, :, q, m], b_recv.at[SIDE * f + j])
                ct[k, own, m] = ct[k, own, m] + afirst[f, 0, q, m] + afirst[f, 1, q, m] + afirst[f, 2, q, m]
                for core in (0, 1):
                    if j or core:
                        at = 2 * j + core - 1
                        part = pl.ds(pl.multiple_of(shifted(z, j) * MZ + ((c + core) % 2) * (MZ // 2), MZ // 2), MZ // 2)
                        go(remote(ct.at[k, own, part], zdirect.at[f, at, q], d_send.at[f], d_recv.at[f],
                                  device(a, b, shifted(z, j), (c + core) % 2)))
            wait_sent(zdirect.at[f, :, q], d_send.at[f])

    def write(k, value):
        rows = pl.ds(starts[k], CHUNKS[k])
        o_ref[rows, :] = value

    def reduce_second(k):
        size = CHUNKS[k]
        rows = pl.ds(starts[k], size)
        own = pl.ds(pl.multiple_of(a * size, size), size)
        q = pl.ds(0, size)
        if z_first[k]:
            wait_received(abuf.at[k, :, q], a_recv.at[k])
            asum[rows, :] = zs[k, own, :] + abuf[k, 0, q, :] + abuf[k, 1, q, :] + abuf[k, 2, q, :]
            c_copies[k] = go(remote(asum.at[rows, half(1 - c)], cbuf.at[rows], c_send.at[k], c_recv.at[k], other_core))
            sent.append(c_copies[k])

    def finish(k):
        size = CHUNKS[k]
        rows = pl.ds(starts[k], size)
        q = pl.ds(0, size)
        if z_first[k]:
            c_copies[k].wait_recv()
            write(k, asum[rows, half(c)] + cbuf[rows, :])
        else:
            f = k - last + A_FIRST
            own = pl.ds(pl.multiple_of(a * size, size), size)
            value = ct[k, own, pl.ds(pl.multiple_of(z * MZ + c * (MZ // 2), MZ // 2), MZ // 2)]
            wait_received(zdirect.at[f, :, q], d_recv.at[f])
            for at in range(7):
                value += zdirect[f, at, q, :]
            write(k, value)

    gather(0, t_ref.at[:, columns(a)])
    send_v(0)
    t_copies[1].wait_recv()
    gather(1, tbuf.at[slot(b, shifted(a, -1))])
    t_copies[3].wait_recv()
    gather(3, tbuf.at[slot(b, shifted(a, -3))])
    forward(0)
    t_copies[2].wait_recv()
    gather(2, tbuf.at[slot(b, shifted(a, -2))])
    t_own.wait()
    v_own.wait()
    pl.loop(0, SIDE)(lambda j: convert_t(b, shifted(a, -j)))
    forward(1)
    forward(3)
    forward(2)
    send_v(1)
    pl.loop(0, SIDE)(convert_sides)
    convert_v(0)
    early_tiles()

    for k in range(1, last):
        for later in range(2 if k == 1 else k + 2, min(k + 3, last)):
            send_v(later)
        all_tiles(k)
        if 2 <= k < last - A_FIRST + 1:
            reduce_first(k - 2)
    for k in range(last - A_FIRST - 1, last):
        reduce_first(k)
    for k in range(last):
        reduce_second(k)
    for k in range(last):
        finish(k)
    for copy in sent:
        copy.wait_send()


def local(amplitudes, integrals):
    steps, most = len(CHUNKS), max(CHUNKS)
    bf16, f32 = jnp.bfloat16, jnp.float32
    dma = pltpu.SemaphoreType.DMA
    return pl.pallas_call(
        kernel,
        out_shape=pltpu.VMEM((VROWS, MZ // 2), f32),
        in_specs=[pl.BlockSpec(memory_space=pl.ANY)] * 2,
        out_specs=pl.BlockSpec(memory_space=pltpu.VMEM),
        scratch_shapes=[
            pltpu.VMEM((SIDE * SIDE, TROWS, KQ), f32),
            pltpu.VMEM((SIDE, VROWS, KQ), f32),
            pltpu.VMEM((SIDE * SIDE * TROWS, KQ), bf16),
            pltpu.VMEM((SIDE * SIDE * TROWS, KQ), bf16),
            pltpu.VMEM((2 * SIDE * most, KQ), bf16),
            pltpu.VMEM((steps, SIDE * most, SIDE * MZ), f32),
            pltpu.VMEM((steps, SIDE - 1, SIDE * most, MZ), f32),
            pltpu.VMEM((steps, SIDE * most, MZ), f32),
            pltpu.VMEM((steps, SIDE - 1, most, MZ), f32),
            pltpu.VMEM((A_FIRST, SIDE - 1, most, SIDE * MZ), f32),
            pltpu.VMEM((A_FIRST, 7, most, MZ // 2), f32),
            pltpu.VMEM((VROWS, MZ), f32),
            pltpu.VMEM((VROWS, MZ // 2), f32),
            dma(()), dma((SIDE - 1,)),
            dma(()), dma((2 * SIDE,)),
            dma(()), dma((SIDE,)),
            dma(()), dma((steps,)),
            dma((steps - A_FIRST,)), dma((steps - A_FIRST,)),
            dma((steps - A_FIRST,)), dma((steps - A_FIRST,)),
            dma((A_FIRST,)), dma((A_FIRST,)),
            dma((A_FIRST,)), dma((SIDE * A_FIRST,)),
            dma((steps - A_FIRST,)), dma((steps - A_FIRST,)),
            dma((2,)),
        ],
        compiler_params=pltpu.CompilerParams(collective_id=0, has_side_effects=True, vmem_limit_bytes=VMEM_BYTES),
        cost_estimate=pl.CostEstimate(flops=3 * 2 * 1024 * 1024 * KQ, bytes_accessed=10 << 20, transcendentals=0),
    )(amplitudes, integrals).T


def solution(mesh):
    in_specs = (P("ab", "ij"), P("ab", "ij"))
    out_specs = P("ij", "ab")
    return jax.shard_map(local, mesh=mesh, in_specs=in_specs, out_specs=out_specs, check_vma=False)
```

```python
import functools

import jax
import jax.numpy as jnp
from jax import lax
from jax.experimental import pallas as pl
from jax.experimental.pallas import tpu as pltpu
from jax.sharding import PartitionSpec as P

SIDE = 4
KQ = 2048
TROWS = 64
VROWS = 256
MZ = 256
CHUNKS = (64, 64, 64, 32, 32)
LATE = 1
A_FIRST = 2
VMEM_BYTES = 60 << 20


def place():
    ij, ab = lax.axis_index("ij"), lax.axis_index("ab")
    return ab % SIDE, ab // SIDE, ij // 2, ij % 2


def dot_nt(left, right):
    return lax.dot_general(left, right, (((1,), (1,)), ((), ())), preferred_element_type=jnp.float32)


def split(value):
    high = value.astype(jnp.bfloat16)
    return high, (value - high.astype(jnp.float32)).astype(jnp.bfloat16)


def kernel(t_ref, v_ref, o_ref, tbuf, vbuf, thi, tlo, vhl, ct, zh, zbuf, zs, abuf, afirst, zdirect,
           t_send, t_recv, g_send, g_recv, f_send, f_recv, v_send, v_recv, z_send, z_recv, a_send, a_recv,
           d_send, d_recv, b_send, b_recv, h_send, h_recv, local_sem):
    x, y, z, c = place()
    a = x * (1 - c) + y * c
    b = y * (1 - c) + x * c

    def device(a_to, b_to, z_to, c_to):
        x_to = a_to * (1 - c) + b_to * c
        y_to = b_to * (1 - c) + a_to * c
        return (z_to * 2 + c_to, y_to * SIDE + x_to)

    def slot(b_of, a_of):
        return (b_of * (1 - c) + a_of * c) * SIDE + a_of * (1 - c) + b_of * c

    def shifted(position, by):
        return (position + by + SIDE) % SIDE

    def along_a(by):
        return device(shifted(a, by), b, z, c)

    def along_b(by):
        return device(a, shifted(b, by), z, c)

    def along_z(by):
        return device(a, b, shifted(z, by), c)

    other_core = (z * 2 + 1 - c, y * SIDE + x)

    def columns(of):
        return pl.ds(pl.multiple_of(of * KQ, KQ), KQ)

    def remote(src, dst, send, recv, to):
        return pltpu.make_async_remote_copy(src_ref=src, dst_ref=dst, send_sem=send, recv_sem=recv, device_id=to,
                                            device_id_type=pl.DeviceIdType.MESH)

    barrier = pltpu.get_barrier_semaphore()
    peers = [along_a(j) for j in (1, 2, 3)] + [along_b(1), along_b(-1)] + [along_z(j) for j in (1, 2, 3)] + [other_core]
    peers += [device(a, b, shifted(z, j), 1 - c) for j in (1, 2, 3)]
    peers += [device(a, shifted(b, j), z, 1 - c) for j in (1, 2, 3)]
    for peer in peers:
        pl.semaphore_signal(barrier, inc=1, device_id=peer, device_id_type=pl.DeviceIdType.MESH)
    pl.semaphore_wait(barrier, len(peers))

    sent = []

    def go(copy):
        copy.start()
        return copy

    def wait_sent(like, sem):
        sent.append(remote(like, like, sem, sem, other_core))

    def wait_received(like, sem):
        remote(like, like, sem, sem, other_core).wait_recv()

    t_copies = {}
    for j in (1, 3, 2):
        t_copies[j] = go(remote(t_ref.at[:, columns(shifted(a, j))], tbuf.at[slot(b, a)], t_send, t_recv.at[j - 1], along_a(j)))
    wait_sent(vbuf.at[0, pl.ds(0, 3 * TROWS)], t_send)
    t_own = pltpu.make_async_copy(t_ref.at[:, columns(a)], tbuf.at[slot(b, a)], local_sem.at[0])
    t_own.start()
    v_own = pltpu.make_async_copy(v_ref.at[:, columns(a)], vbuf.at[a], local_sem.at[1])
    v_own.start()

    g_copies = {}
    wait_sent(vbuf.at[pl.ds(0, 2)], g_send)
    wait_sent(vbuf.at[0], f_send)

    def gather(j, src):
        dst = tbuf.at[slot(b, shifted(a, -j))]
        g_copies[j] = [go(remote(src, dst, g_send, g_recv.at[2 * j + w], along_b(by))) for w, by in ((0, 1), (1, -1))]

    def f_copy(j, w):
        by = 1 - 2 * w
        part = tbuf.at[slot(shifted(b, -by), shifted(a, -j)), pl.ds(w * (TROWS // 2), TROWS // 2)]
        return remote(part, part, f_send, f_recv.at[j], along_b(by))

    def forward(j):
        for w in (0, 1):
            g_copies[j][w].wait_recv()
            go(f_copy(j, w))

    wait_sent(vbuf.at[pl.ds(0, 3)], v_send)
    starts = [sum(CHUNKS[:k]) for k in range(len(CHUNKS))]

    def send_v(k):
        rows = pl.ds(starts[k], CHUNKS[k])
        for j in (1, 3, 2):
            go(remote(v_ref.at[rows, columns(shifted(a, j))], vbuf.at[a, rows], v_send, v_recv.at[k], along_a(j)))

    def send_v_half(h):
        k = len(CHUNKS) - 1
        rows = pl.ds(starts[k], CHUNKS[k])
        for j in (1, 3, 2):
            src = pl.ds(pl.multiple_of(shifted(a, j) * KQ + h * (KQ // 2), KQ // 2), KQ // 2)
            go(remote(v_ref.at[rows, src], vbuf.at[a, rows, pl.ds(h * (KQ // 2), KQ // 2)], v_send, v_recv.at[k + h], along_a(j)))

    def convert_t(b_of, a_of):
        s = slot(b_of, a_of)
        rows = pl.ds(pl.multiple_of(s * TROWS, TROWS), TROWS)
        thi[rows, :], tlo[rows, :] = split(tbuf[s])

    def convert_sides(j):
        for by in (1, -1):
            convert_t(shifted(b, -by), shifted(a, -j))


    def lanes_of(z_of):
        return pl.ds(pl.multiple_of(z_of * MZ, MZ), MZ)

    def half(core):
        return pl.ds(pl.multiple_of(core * (MZ // 2), MZ // 2), MZ // 2)

    last = len(CHUNKS)
    z_first = [k < last - A_FIRST for k in range(last)]

    def convert_v(k):
        size = CHUNKS[k]
        n = SIDE * size
        wait_received(vbuf.at[pl.ds(0, 3), pl.ds(starts[k], size)], v_recv.at[k])

        @pl.loop(0, SIDE)
        def _(s):
            high, low = pl.ds(pl.multiple_of(s * size, size), size), pl.ds(pl.multiple_of(n + s * size, size), size)
            vhl[high, :], vhl[low, :] = split(vbuf[s, pl.ds(starts[k], size), :])

    def multiply(k, m):
        n = SIDE * CHUNKS[k]
        both = dot_nt(vhl[pl.ds(0, 2 * n), :], thi[m, :])
        ct[k, pl.ds(0, n), m] = both[:n] + both[n:] + dot_nt(vhl[pl.ds(0, n), :], tlo[m, :])

    def z_copy(k, j):
        n = pl.ds(0, SIDE * CHUNKS[k])
        return remote(ct.at[k, n, lanes_of(shifted(z, j))], zbuf.at[k, j - 1, n], z_send.at[k], z_recv.at[k], along_z(j))

    def early_tiles():
        @pl.loop(0, SIDE)
        def _(i):
            j = i + i // 2 - 2 * (i // 3)
            wait_received(tbuf.at[0], f_recv.at[j])
            convert_t(shifted(b, 2), shifted(a, -j))
            z_of = shifted(y, -j)
            multiply(0, lanes_of(z_of))
            by = shifted(z_of, -z)

            @pl.when(by != 0)
            def _():
                z_copy(0, by).start()

        wait_sent(zbuf.at[0, :, pl.ds(0, SIDE * CHUNKS[0])], z_send.at[0])

    def a_first_copy(k, j, i):
        size, f = CHUNKS[k], k - last + A_FIRST
        m = lanes_of(shifted(z, j))
        part = pl.ds(pl.multiple_of(shifted(a, i) * size, size), size)
        return remote(ct.at[k, part, m], afirst.at[f, i - 1, pl.ds(0, size), m], b_send.at[f],
                      b_recv.at[SIDE * f + j], along_a(i))

    def half_tiles(k, h):
        size = CHUNKS[k]
        n = SIDE * size
        lanes = pl.ds(h * (KQ // 2), KQ // 2)
        wait_received(vbuf.at[pl.ds(0, 3), pl.ds(starts[k], size), lanes], v_recv.at[k + h])

        @pl.loop(0, SIDE)
        def _(s):
            high, low = pl.ds(pl.multiple_of(s * size, size), size), pl.ds(pl.multiple_of(n + s * size, size), size)
            vhl[high, lanes], vhl[low, lanes] = split(vbuf[s, pl.ds(starts[k], size), lanes])

        @pl.loop(0, SIDE)
        def _(step):
            j = (step + 1) % SIDE
            m = lanes_of(shifted(z, j))
            both = dot_nt(vhl[pl.ds(0, 2 * n), lanes], thi[m, lanes])
            value = both[:n] + both[n:] + dot_nt(vhl[pl.ds(0, n), lanes], tlo[m, lanes])
            if h == 0:
                ct[k, pl.ds(0, n), m] = value
            else:
                ct[k, pl.ds(0, n), m] += value
                for i in (2, 1, 3):
                    a_first_copy(k, j, i).start()

    def all_tiles(k):
        if k == last - 1:
            half_tiles(k, 0)
            half_tiles(k, 1)
            wait_sent(afirst.at[k - last + A_FIRST, :, pl.ds(0, CHUNKS[k])], b_send.at[k - last + A_FIRST])
            return
        convert_v(k)

        n = SIDE * CHUNKS[k]

        def opposite_half(w):
            part = ct.at[k, pl.ds(w * n // 2, n // 2), lanes_of(shifted(z, 2))]
            return remote(part, zh.at[k, w, pl.ds(0, n // 2)], h_send.at[k], h_recv.at[k], along_z(1 - 2 * w))

        @pl.loop(0, SIDE)
        def _(step):
            j = (step + 2) % SIDE if z_first[k] else (step + 1) % SIDE
            multiply(k, lanes_of(shifted(z, j)))
            if z_first[k]:
                @pl.when(step == 0)
                def _():
                    for w in (0, 1):
                        opposite_half(w).start()
            else:
                for i in (2, 1, 3):
                    a_first_copy(k, j, i).start()

        if z_first[k]:
            wait_sent(zh.at[k, :, pl.ds(0, n // 2)], h_send.at[k])
            wait_received(zh.at[k, :, pl.ds(0, n // 2)], h_recv.at[k])
            for w in (0, 1):
                m = lanes_of(shifted(z, 1 - 2 * w))
                rows = pl.ds(0, n)
                ct[k, pl.ds(w * n // 2, n // 2), m] += zh[k, w, pl.ds(0, n // 2), :]
                go(remote(ct.at[k, rows, m], zbuf.at[k, w, rows], z_send.at[k], z_recv.at[k], along_z(1 - 2 * w)))
            wait_sent(zbuf.at[k, pl.ds(0, 2), pl.ds(0, n)], z_send.at[k])
        else:
            f = k - last + A_FIRST
            wait_sent(afirst.at[f, :, pl.ds(0, CHUNKS[k])], b_send.at[f])

    def reduce_first(k):
        size = CHUNKS[k]
        q = pl.ds(0, size)
        if z_first[k]:
            n = pl.ds(0, SIDE * size)
            pieces = 2 if k else 3
            wait_received(zbuf.at[k, pl.ds(0, pieces), n], z_recv.at[k])
            value = ct[k, n, lanes_of(z)]
            for at in range(pieces):
                value += zbuf[k, at, n, :]
            zs[k, n, :] = value
            for j in (2, 1, 3, 0):
                part = pl.ds(pl.multiple_of(shifted(a, j) * size, size), size)
                for core in (0, 1):
                    if j or core:
                        to = device(shifted(a, j), b, z, (c + core) % 2)
                        go(remote(zs.at[k, part, half((c + core) % 2)], abuf.at[k, 2 * j + core - 1, q], a_send.at[k], a_recv.at[k], to))
            wait_sent(abuf.at[k, :, q], a_send.at[k])
        else:
            f = k - last + A_FIRST
            own = pl.ds(pl.multiple_of(a * size, size), size)
            for j in (1, 2, 3, 0):
                m = lanes_of(shifted(z, j))
                wait_received(afirst.at[f, :, q, m], b_recv.at[SIDE * f + j])
                ct[k, own, m] = ct[k, own, m] + afirst[f, 0, q, m] + afirst[f, 1, q, m] + afirst[f, 2, q, m]
                for core in (0, 1):
                    if j or core:
                        at = 2 * j + core - 1
                        part = pl.ds(pl.multiple_of(shifted(z, j) * MZ + ((c + core) % 2) * (MZ // 2), MZ // 2), MZ // 2)
                        go(remote(ct.at[k, own, part], zdirect.at[f, at, q], d_send.at[f], d_recv.at[f],
                                  device(a, b, shifted(z, j), (c + core) % 2)))
            wait_sent(zdirect.at[f, :, q], d_send.at[f])

    def write(k, value):
        rows = pl.ds(starts[k], CHUNKS[k])
        o_ref[rows, :] = value

    def finish(k):
        size = CHUNKS[k]
        own = pl.ds(pl.multiple_of(a * size, size), size)
        q = pl.ds(0, size)
        if z_first[k]:
            parts, at_k, recv, value = abuf, k, a_recv, zs[k, own, half(c)]
        else:
            f = k - last + A_FIRST
            parts, at_k, recv = zdirect, f, d_recv
            value = ct[k, own, pl.ds(pl.multiple_of(z * MZ + c * (MZ // 2), MZ // 2), MZ // 2)]
        wait_received(parts.at[at_k, :, q], recv.at[at_k])
        for at in range(7):
            value += parts[at_k, at, q, :]
        o_ref[pl.ds(starts[k], size), :] = value

    gather(0, t_ref.at[:, columns(a)])
    send_v(0)
    t_copies[1].wait_recv()
    gather(1, tbuf.at[slot(b, shifted(a, -1))])
    t_copies[3].wait_recv()
    gather(3, tbuf.at[slot(b, shifted(a, -3))])
    forward(0)
    t_copies[2].wait_recv()
    gather(2, tbuf.at[slot(b, shifted(a, -2))])
    t_own.wait()
    v_own.wait()
    pl.loop(0, SIDE)(lambda j: convert_t(b, shifted(a, -j)))
    forward(1)
    forward(3)
    forward(2)
    send_v(1)
    pl.loop(0, SIDE)(convert_sides)
    convert_v(0)
    early_tiles()

    for k in range(1, last):
        for later in range(2 if k == 1 else k + 2, min(k + 3, last)):
            if later < last - 1:
                send_v(later)
        if k == last - 3:
            send_v_half(0)
        if k == last - 2 - LATE:
            send_v_half(1)
        all_tiles(k)
        if 2 <= k < last - A_FIRST + 1:
            reduce_first(k - 2)
    for k in range(last - A_FIRST - 1, last):
        reduce_first(k)
    for k in range(last):
        finish(k)
    for copy in sent:
        copy.wait_send()


def local(amplitudes, integrals):
    steps, most = len(CHUNKS), max(CHUNKS)
    bf16, f32 = jnp.bfloat16, jnp.float32
    dma = pltpu.SemaphoreType.DMA
    return pl.pallas_call(
        kernel,
        out_shape=pltpu.VMEM((VROWS, MZ // 2), f32),
        in_specs=[pl.BlockSpec(memory_space=pl.ANY)] * 2,
        out_specs=pl.BlockSpec(memory_space=pltpu.VMEM),
        scratch_shapes=[
            pltpu.VMEM((SIDE * SIDE, TROWS, KQ), f32),
            pltpu.VMEM((SIDE, VROWS, KQ), f32),
            pltpu.VMEM((SIDE * SIDE * TROWS, KQ), bf16),
            pltpu.VMEM((SIDE * SIDE * TROWS, KQ), bf16),
            pltpu.VMEM((2 * SIDE * most, KQ), bf16),
            pltpu.VMEM((steps, SIDE * most, SIDE * MZ), f32),
            pltpu.VMEM((steps, 2, SIDE * most // 2, MZ), f32),
            pltpu.VMEM((steps, SIDE - 1, SIDE * most, MZ), f32),
            pltpu.VMEM((steps, SIDE * most, MZ), f32),
            pltpu.VMEM((steps, 7, most, MZ // 2), f32),
            pltpu.VMEM((A_FIRST, SIDE - 1, most, SIDE * MZ), f32),
            pltpu.VMEM((A_FIRST, 7, most, MZ // 2), f32),
            dma(()), dma((SIDE - 1,)),
            dma(()), dma((2 * SIDE,)),
            dma(()), dma((SIDE,)),
            dma(()), dma((steps + 1,)),
            dma((steps - A_FIRST,)), dma((steps - A_FIRST,)),
            dma((steps - A_FIRST,)), dma((steps - A_FIRST,)),
            dma((A_FIRST,)), dma((A_FIRST,)),
            dma((A_FIRST,)), dma((SIDE * A_FIRST,)),
            dma((steps - A_FIRST,)), dma((steps - A_FIRST,)),
            dma((2,)),
        ],
        compiler_params=pltpu.CompilerParams(collective_id=0, has_side_effects=True, vmem_limit_bytes=VMEM_BYTES),
        cost_estimate=pl.CostEstimate(flops=3 * 2 * 1024 * 1024 * KQ, bytes_accessed=10 << 20, transcendentals=0),
    )(amplitudes, integrals).T


def solution(mesh):
    in_specs = (P("ab", "ij"), P("ab", "ij"))
    out_specs = P("ij", "ab")
    return jax.shard_map(local, mesh=mesh, in_specs=in_specs, out_specs=out_specs, check_vma=False)
```

```python
import functools

import jax
import jax.numpy as jnp
from jax import lax
from jax.experimental import pallas as pl
from jax.experimental.pallas import tpu as pltpu
from jax.sharding import PartitionSpec as P

SIDE = 4
KQ = 2048
TROWS = 64
VROWS = 256
MZ = 256
CHUNKS = (64, 64, 48, 48, 32)
LATE = 1
DELAY = 1
A_FIRST = 2
VMEM_BYTES = 60 << 20


def place():
    ij, ab = lax.axis_index("ij"), lax.axis_index("ab")
    return ab % SIDE, ab // SIDE, ij // 2, ij % 2


def dot_nt(left, right):
    return lax.dot_general(left, right, (((1,), (1,)), ((), ())), preferred_element_type=jnp.float32)


def split(value):
    high = value.astype(jnp.bfloat16)
    return high, (value - high.astype(jnp.float32)).astype(jnp.bfloat16)


def kernel(t_ref, v_ref, o_ref, tbuf, vbuf, thi, tlo, vhl, ct, zh, zbuf, zs, abuf, afirst, zdirect,
           t_send, t_recv, g_send, g_recv, f_send, f_recv, v_send, v_recv, z_send, z_recv, a_send, a_recv,
           d_send, d_recv, b_send, b_recv, h_send, h_recv, local_sem):
    x, y, z, c = place()
    a = x * (1 - c) + y * c
    b = y * (1 - c) + x * c

    def device(a_to, b_to, z_to, c_to):
        x_to = a_to * (1 - c) + b_to * c
        y_to = b_to * (1 - c) + a_to * c
        return (z_to * 2 + c_to, y_to * SIDE + x_to)

    def slot(b_of, a_of):
        return (b_of * (1 - c) + a_of * c) * SIDE + a_of * (1 - c) + b_of * c

    def shifted(position, by):
        return (position + by + SIDE) % SIDE

    def along_a(by):
        return device(shifted(a, by), b, z, c)

    def along_b(by):
        return device(a, shifted(b, by), z, c)

    def along_z(by):
        return device(a, b, shifted(z, by), c)

    other_core = (z * 2 + 1 - c, y * SIDE + x)

    def columns(of):
        return pl.ds(pl.multiple_of(of * KQ, KQ), KQ)

    def remote(src, dst, send, recv, to):
        return pltpu.make_async_remote_copy(src_ref=src, dst_ref=dst, send_sem=send, recv_sem=recv, device_id=to,
                                            device_id_type=pl.DeviceIdType.MESH)

    barrier = pltpu.get_barrier_semaphore()
    peers = [along_a(j) for j in (1, 2, 3)] + [along_b(1), along_b(-1)] + [along_z(j) for j in (1, 2, 3)] + [other_core]
    peers += [device(a, b, shifted(z, j), 1 - c) for j in (1, 2, 3)]
    peers += [device(a, shifted(b, j), z, 1 - c) for j in (1, 2, 3)]
    for peer in peers:
        pl.semaphore_signal(barrier, inc=1, device_id=peer, device_id_type=pl.DeviceIdType.MESH)
    pl.semaphore_wait(barrier, len(peers))

    sent = []

    def go(copy):
        copy.start()
        return copy

    def wait_sent(like, sem):
        sent.append(remote(like, like, sem, sem, other_core))

    def wait_received(like, sem):
        remote(like, like, sem, sem, other_core).wait_recv()

    t_copies = {}
    for j in (1, 3, 2):
        t_copies[j] = go(remote(t_ref.at[:, columns(shifted(a, j))], tbuf.at[slot(b, a)], t_send, t_recv.at[j - 1], along_a(j)))
    wait_sent(vbuf.at[0, pl.ds(0, 3 * TROWS)], t_send)
    t_own = pltpu.make_async_copy(t_ref.at[:, columns(a)], tbuf.at[slot(b, a)], local_sem.at[0])
    t_own.start()
    v_own = pltpu.make_async_copy(v_ref.at[:, columns(a)], vbuf.at[a], local_sem.at[1])
    v_own.start()

    g_copies = {}
    wait_sent(vbuf.at[pl.ds(0, 2)], g_send)
    wait_sent(vbuf.at[0], f_send)

    def gather(j, src):
        dst = tbuf.at[slot(b, shifted(a, -j))]
        g_copies[j] = [go(remote(src, dst, g_send, g_recv.at[2 * j + w], along_b(by))) for w, by in ((0, 1), (1, -1))]

    def f_copy(j, w):
        by = 1 - 2 * w
        part = tbuf.at[slot(shifted(b, -by), shifted(a, -j)), pl.ds(w * (TROWS // 2), TROWS // 2)]
        return remote(part, part, f_send, f_recv.at[j], along_b(by))

    def forward(j):
        for w in (0, 1):
            g_copies[j][w].wait_recv()
            go(f_copy(j, w))

    wait_sent(vbuf.at[pl.ds(0, 3)], v_send)
    starts = [sum(CHUNKS[:k]) for k in range(len(CHUNKS))]

    def send_v(k):
        rows = pl.ds(starts[k], CHUNKS[k])
        for j in (1, 3, 2):
            go(remote(v_ref.at[rows, columns(shifted(a, j))], vbuf.at[a, rows], v_send, v_recv.at[k], along_a(j)))

    def send_v_half(h):
        k = len(CHUNKS) - 1
        rows = pl.ds(starts[k], CHUNKS[k])
        for j in (1, 3, 2):
            src = pl.ds(pl.multiple_of(shifted(a, j) * KQ + h * (KQ // 2), KQ // 2), KQ // 2)
            go(remote(v_ref.at[rows, src], vbuf.at[a, rows, pl.ds(h * (KQ // 2), KQ // 2)], v_send, v_recv.at[k + h], along_a(j)))

    def convert_t(b_of, a_of):
        s = slot(b_of, a_of)
        rows = pl.ds(pl.multiple_of(s * TROWS, TROWS), TROWS)
        thi[rows, :], tlo[rows, :] = split(tbuf[s])

    def convert_sides(j):
        for by in (1, -1):
            convert_t(shifted(b, -by), shifted(a, -j))


    def lanes_of(z_of):
        return pl.ds(pl.multiple_of(z_of * MZ, MZ), MZ)

    def half(core):
        return pl.ds(pl.multiple_of(core * (MZ // 2), MZ // 2), MZ // 2)

    last = len(CHUNKS)
    z_first = [k < last - A_FIRST for k in range(last)]

    def convert_v(k):
        size = CHUNKS[k]
        n = SIDE * size
        wait_received(vbuf.at[pl.ds(0, 3), pl.ds(starts[k], size)], v_recv.at[k])

        @pl.loop(0, SIDE)
        def _(s):
            high, low = pl.ds(pl.multiple_of(s * size, size), size), pl.ds(pl.multiple_of(n + s * size, size), size)
            vhl[high, :], vhl[low, :] = split(vbuf[s, pl.ds(starts[k], size), :])

    def multiply(k, m):
        n = SIDE * CHUNKS[k]
        both = dot_nt(vhl[pl.ds(0, 2 * n), :], thi[m, :])
        ct[k, pl.ds(0, n), m] = both[:n] + both[n:] + dot_nt(vhl[pl.ds(0, n), :], tlo[m, :])

    def z_copy(k, j):
        n = pl.ds(0, SIDE * CHUNKS[k])
        return remote(ct.at[k, n, lanes_of(shifted(z, j))], zbuf.at[k, j - 1, n], z_send.at[k], z_recv.at[k], along_z(j))

    def early_tiles():
        @pl.loop(0, SIDE)
        def _(i):
            j = i + i // 2 - 2 * (i // 3)
            wait_received(tbuf.at[0], f_recv.at[j])
            convert_t(shifted(b, 2), shifted(a, -j))
            z_of = shifted(y, -j)
            multiply(0, lanes_of(z_of))
            by = shifted(z_of, -z)

            @pl.when(by != 0)
            def _():
                z_copy(0, by).start()

        wait_sent(zbuf.at[0, :, pl.ds(0, SIDE * CHUNKS[0])], z_send.at[0])

    def a_first_copy(k, j, i):
        size, f = CHUNKS[k], k - last + A_FIRST
        m = lanes_of(shifted(z, j))
        part = pl.ds(pl.multiple_of(shifted(a, i) * size, size), size)
        return remote(ct.at[k, part, m], afirst.at[f, i - 1, pl.ds(0, size), m], b_send.at[f],
                      b_recv.at[SIDE * f + j], along_a(i))

    def half_tiles(k, h):
        size = CHUNKS[k]
        n = SIDE * size
        lanes = pl.ds(h * (KQ // 2), KQ // 2)
        wait_received(vbuf.at[pl.ds(0, 3), pl.ds(starts[k], size), lanes], v_recv.at[k + h])

        @pl.loop(0, SIDE)
        def _(s):
            high, low = pl.ds(pl.multiple_of(s * size, size), size), pl.ds(pl.multiple_of(n + s * size, size), size)
            vhl[high, lanes], vhl[low, lanes] = split(vbuf[s, pl.ds(starts[k], size), lanes])

        @pl.loop(0, SIDE)
        def _(step):
            j = (step + 1) % SIDE
            m = lanes_of(shifted(z, j))
            both = dot_nt(vhl[pl.ds(0, 2 * n), lanes], thi[m, lanes])
            value = both[:n] + both[n:] + dot_nt(vhl[pl.ds(0, n), lanes], tlo[m, lanes])
            if h == 0:
                ct[k, pl.ds(0, n), m] = value
            else:
                ct[k, pl.ds(0, n), m] += value
                for i in (2, 1, 3):
                    a_first_copy(k, j, i).start()

    def all_tiles(k):
        if k == last - 1:
            half_tiles(k, 0)
            half_tiles(k, 1)
            wait_sent(afirst.at[k - last + A_FIRST, :, pl.ds(0, CHUNKS[k])], b_send.at[k - last + A_FIRST])
            return
        convert_v(k)

        n = SIDE * CHUNKS[k]

        def opposite_half(w):
            part = ct.at[k, pl.ds(w * n // 2, n // 2), lanes_of(shifted(z, 2))]
            return remote(part, zh.at[k, w, pl.ds(0, n // 2)], h_send.at[k], h_recv.at[k], along_z(1 - 2 * w))

        @pl.loop(0, SIDE)
        def _(step):
            j = (step + 2) % SIDE if z_first[k] else (step + 1) % SIDE
            multiply(k, lanes_of(shifted(z, j)))
            if z_first[k]:
                @pl.when(step == 0)
                def _():
                    for w in (0, 1):
                        opposite_half(w).start()
            else:
                for i in (2, 1, 3):
                    a_first_copy(k, j, i).start()

        if z_first[k]:
            wait_sent(zh.at[k, :, pl.ds(0, n // 2)], h_send.at[k])
        else:
            f = k - last + A_FIRST
            wait_sent(afirst.at[f, :, pl.ds(0, CHUNKS[k])], b_send.at[f])

    def onward_z(k):
        n = SIDE * CHUNKS[k]
        wait_received(zh.at[k, :, pl.ds(0, n // 2)], h_recv.at[k])
        for w in (0, 1):
            m = lanes_of(shifted(z, 1 - 2 * w))
            rows = pl.ds(0, n)
            ct[k, pl.ds(w * n // 2, n // 2), m] += zh[k, w, pl.ds(0, n // 2), :]
            go(remote(ct.at[k, rows, m], zbuf.at[k, w, rows], z_send.at[k], z_recv.at[k], along_z(1 - 2 * w)))
        wait_sent(zbuf.at[k, pl.ds(0, 2), pl.ds(0, n)], z_send.at[k])

    def reduce_first(k):
        size = CHUNKS[k]
        q = pl.ds(0, size)
        if z_first[k]:
            n = pl.ds(0, SIDE * size)
            pieces = 2 if k else 3
            wait_received(zbuf.at[k, pl.ds(0, pieces), n], z_recv.at[k])
            value = ct[k, n, lanes_of(z)]
            for at in range(pieces):
                value += zbuf[k, at, n, :]
            zs[k, n, :] = value
            for j in (2, 1, 3, 0):
                part = pl.ds(pl.multiple_of(shifted(a, j) * size, size), size)
                for core in (0, 1):
                    if j or core:
                        to = device(shifted(a, j), b, z, (c + core) % 2)
                        go(remote(zs.at[k, part, half((c + core) % 2)], abuf.at[k, 2 * j + core - 1, q], a_send.at[k], a_recv.at[k], to))
            wait_sent(abuf.at[k, :, q], a_send.at[k])
        else:
            f = k - last + A_FIRST
            own = pl.ds(pl.multiple_of(a * size, size), size)
            for j in (1, 2, 3, 0):
                m = lanes_of(shifted(z, j))
                wait_received(afirst.at[f, :, q, m], b_recv.at[SIDE * f + j])
                ct[k, own, m] = ct[k, own, m] + afirst[f, 0, q, m] + afirst[f, 1, q, m] + afirst[f, 2, q, m]
                for core in (0, 1):
                    if j or core:
                        at = 2 * j + core - 1
                        part = pl.ds(pl.multiple_of(shifted(z, j) * MZ + ((c + core) % 2) * (MZ // 2), MZ // 2), MZ // 2)
                        go(remote(ct.at[k, own, part], zdirect.at[f, at, q], d_send.at[f], d_recv.at[f],
                                  device(a, b, shifted(z, j), (c + core) % 2)))
            wait_sent(zdirect.at[f, :, q], d_send.at[f])

    def write(k, value):
        rows = pl.ds(starts[k], CHUNKS[k])
        o_ref[rows, :] = value

    def finish(k):
        size = CHUNKS[k]
        own = pl.ds(pl.multiple_of(a * size, size), size)
        q = pl.ds(0, size)
        if z_first[k]:
            parts, at_k, recv, value = abuf, k, a_recv, zs[k, own, half(c)]
        else:
            f = k - last + A_FIRST
            parts, at_k, recv = zdirect, f, d_recv
            value = ct[k, own, pl.ds(pl.multiple_of(z * MZ + c * (MZ // 2), MZ // 2), MZ // 2)]
        wait_received(parts.at[at_k, :, q], recv.at[at_k])
        for at in range(7):
            value += parts[at_k, at, q, :]
        o_ref[pl.ds(starts[k], size), :] = value

    gather(0, t_ref.at[:, columns(a)])
    send_v(0)
    t_copies[1].wait_recv()
    gather(1, tbuf.at[slot(b, shifted(a, -1))])
    t_copies[3].wait_recv()
    gather(3, tbuf.at[slot(b, shifted(a, -3))])
    forward(0)
    t_copies[2].wait_recv()
    gather(2, tbuf.at[slot(b, shifted(a, -2))])
    t_own.wait()
    v_own.wait()
    pl.loop(0, SIDE)(lambda j: convert_t(b, shifted(a, -j)))
    forward(1)
    forward(3)
    forward(2)
    send_v(1)
    pl.loop(0, SIDE)(convert_sides)
    convert_v(0)
    early_tiles()

    for k in range(1, last):
        for later in range(2 if k == 1 else k + 2, min(k + 3, last)):
            if later < last - 1:
                send_v(later)
        if k == last - 3:
            send_v_half(0)
        if k == last - 2 - LATE:
            send_v_half(1)
        all_tiles(k)
        if k < last - A_FIRST and not (DELAY and k == last - A_FIRST - 1):
            onward_z(k)
        if DELAY and k == last - A_FIRST:
            onward_z(k - 1)
    for k in [0, 1, last - 2, last - 3, last - 1]:
        reduce_first(k)
    for k in range(last):
        finish(k)
    for copy in sent:
        copy.wait_send()


def local(amplitudes, integrals):
    steps, most = len(CHUNKS), max(CHUNKS)
    bf16, f32 = jnp.bfloat16, jnp.float32
    dma = pltpu.SemaphoreType.DMA
    return pl.pallas_call(
        kernel,
        out_shape=pltpu.VMEM((VROWS, MZ // 2), f32),
        in_specs=[pl.BlockSpec(memory_space=pl.ANY)] * 2,
        out_specs=pl.BlockSpec(memory_space=pltpu.VMEM),
        scratch_shapes=[
            pltpu.VMEM((SIDE * SIDE, TROWS, KQ), f32),
            pltpu.VMEM((SIDE, VROWS, KQ), f32),
            pltpu.VMEM((SIDE * SIDE * TROWS, KQ), bf16),
            pltpu.VMEM((SIDE * SIDE * TROWS, KQ), bf16),
            pltpu.VMEM((2 * SIDE * most, KQ), bf16),
            pltpu.VMEM((steps, SIDE * most, SIDE * MZ), f32),
            pltpu.VMEM((steps, 2, SIDE * most // 2, MZ), f32),
            pltpu.VMEM((steps, SIDE - 1, SIDE * most, MZ), f32),
            pltpu.VMEM((steps, SIDE * most, MZ), f32),
            pltpu.VMEM((steps, 7, most, MZ // 2), f32),
            pltpu.VMEM((A_FIRST, SIDE - 1, most, SIDE * MZ), f32),
            pltpu.VMEM((A_FIRST, 7, most, MZ // 2), f32),
            dma(()), dma((SIDE - 1,)),
            dma(()), dma((2 * SIDE,)),
            dma(()), dma((SIDE,)),
            dma(()), dma((steps + 1,)),
            dma((steps - A_FIRST,)), dma((steps - A_FIRST,)),
            dma((steps - A_FIRST,)), dma((steps - A_FIRST,)),
            dma((A_FIRST,)), dma((A_FIRST,)),
            dma((A_FIRST,)), dma((SIDE * A_FIRST,)),
            dma((steps - A_FIRST,)), dma((steps - A_FIRST,)),
            dma((2,)),
        ],
        compiler_params=pltpu.CompilerParams(collective_id=0, has_side_effects=True, vmem_limit_bytes=VMEM_BYTES),
        cost_estimate=pl.CostEstimate(flops=3 * 2 * 1024 * 1024 * KQ, bytes_accessed=10 << 20, transcendentals=0),
    )(amplitudes, integrals).T


def solution(mesh):
    in_specs = (P("ab", "ij"), P("ab", "ij"))
    out_specs = P("ij", "ab")
    return jax.shard_map(local, mesh=mesh, in_specs=in_specs, out_specs=out_specs, check_vma=False)
```

```python
import functools

import jax
import jax.numpy as jnp
from jax import lax
from jax.experimental import pallas as pl
from jax.experimental.pallas import tpu as pltpu
from jax.sharding import PartitionSpec as P

SIDE = 4
KQ = 2048
TROWS = 64
VROWS = 256
MZ = 256
CHUNKS = (64, 64, 48, 48, 32)
LATE = 1
DELAY = 1
A_FIRST = 2
VMEM_BYTES = 60 << 20


def place():
    ij, ab = lax.axis_index("ij"), lax.axis_index("ab")
    return ab % SIDE, ab // SIDE, ij // 2, ij % 2


def dot_nt(left, right):
    return lax.dot_general(left, right, (((1,), (1,)), ((), ())), preferred_element_type=jnp.float32)


def split(value):
    high = value.astype(jnp.bfloat16)
    return high, (value - high.astype(jnp.float32)).astype(jnp.bfloat16)


def kernel(t_ref, v_ref, o_ref, tbuf, vbuf, thi, tlo, vhl, ct, zh, zbuf, zs, abuf, afirst, zdirect,
           t_send, t_recv, g_send, g_recv, f_send, f_recv, v_send, v_recv, z_send, z_recv, a_send, a_recv,
           d_send, d_recv, b_send, b_recv, h_send, h_recv, local_sem):
    x, y, z, c = place()
    a = x * (1 - c) + y * c
    b = y * (1 - c) + x * c

    def device(a_to, b_to, z_to, c_to):
        x_to = a_to * (1 - c) + b_to * c
        y_to = b_to * (1 - c) + a_to * c
        return (z_to * 2 + c_to, y_to * SIDE + x_to)

    def slot(b_of, a_of):
        return (b_of * (1 - c) + a_of * c) * SIDE + a_of * (1 - c) + b_of * c

    def shifted(position, by):
        return (position + by + SIDE) % SIDE

    def along_a(by):
        return device(shifted(a, by), b, z, c)

    def along_b(by):
        return device(a, shifted(b, by), z, c)

    def along_z(by):
        return device(a, b, shifted(z, by), c)

    other_core = (z * 2 + 1 - c, y * SIDE + x)

    def columns(of):
        return pl.ds(pl.multiple_of(of * KQ, KQ), KQ)

    def remote(src, dst, send, recv, to):
        return pltpu.make_async_remote_copy(src_ref=src, dst_ref=dst, send_sem=send, recv_sem=recv, device_id=to,
                                            device_id_type=pl.DeviceIdType.MESH)

    barrier = pltpu.get_barrier_semaphore()
    peers = [along_a(j) for j in (1, 2, 3)] + [along_b(1), along_b(-1)] + [along_z(j) for j in (1, 2, 3)] + [other_core]
    peers += [device(a, b, shifted(z, j), 1 - c) for j in (1, 2, 3)]
    peers += [device(a, shifted(b, j), z, 1 - c) for j in (1, 2, 3)]
    for peer in peers:
        pl.semaphore_signal(barrier, inc=1, device_id=peer, device_id_type=pl.DeviceIdType.MESH)
    pl.semaphore_wait(barrier, len(peers))

    sent = []

    def go(copy):
        copy.start()
        return copy

    def wait_sent(like, sem):
        sent.append(remote(like, like, sem, sem, other_core))

    def wait_received(like, sem):
        remote(like, like, sem, sem, other_core).wait_recv()

    t_copies = {}
    for j in (1, 3, 2):
        t_copies[j] = go(remote(t_ref.at[:, columns(shifted(a, j))], tbuf.at[slot(b, a)], t_send, t_recv.at[j - 1], along_a(j)))
    wait_sent(vbuf.at[0, pl.ds(0, 3 * TROWS)], t_send)
    t_own = pltpu.make_async_copy(t_ref.at[:, columns(a)], tbuf.at[slot(b, a)], local_sem.at[0])
    t_own.start()
    v_own = pltpu.make_async_copy(v_ref.at[:, columns(a)], vbuf.at[a], local_sem.at[1])
    v_own.start()

    g_copies = {}
    wait_sent(vbuf.at[pl.ds(0, 2)], g_send)
    wait_sent(vbuf.at[0], f_send)

    def gather(j, src):
        dst = tbuf.at[slot(b, shifted(a, -j))]
        g_copies[j] = [go(remote(src, dst, g_send, g_recv.at[2 * j + w], along_b(by))) for w, by in ((0, 1), (1, -1))]

    def f_copy(j, w):
        by = 1 - 2 * w
        part = tbuf.at[slot(shifted(b, -by), shifted(a, -j)), pl.ds(w * (TROWS // 2), TROWS // 2)]
        return remote(part, part, f_send, f_recv.at[j], along_b(by))

    def forward(j):
        for w in (0, 1):
            g_copies[j][w].wait_recv()
            go(f_copy(j, w))

    wait_sent(vbuf.at[pl.ds(0, 3)], v_send)
    starts = [sum(CHUNKS[:k]) for k in range(len(CHUNKS))]

    def send_v(k):
        rows = pl.ds(starts[k], CHUNKS[k])
        for j in (1, 3, 2):
            go(remote(v_ref.at[rows, columns(shifted(a, j))], vbuf.at[a, rows], v_send, v_recv.at[k], along_a(j)))

    def send_v_half(h):
        k = len(CHUNKS) - 1
        rows = pl.ds(starts[k], CHUNKS[k])
        for j in (1, 3, 2):
            src = pl.ds(pl.multiple_of(shifted(a, j) * KQ + h * (KQ // 2), KQ // 2), KQ // 2)
            go(remote(v_ref.at[rows, src], vbuf.at[a, rows, pl.ds(h * (KQ // 2), KQ // 2)], v_send, v_recv.at[k + h], along_a(j)))

    def convert_t(b_of, a_of):
        s = slot(b_of, a_of)
        rows = pl.ds(pl.multiple_of(s * TROWS, TROWS), TROWS)
        thi[rows, :], tlo[rows, :] = split(tbuf[s])

    def convert_sides(j):
        for by in (1, -1):
            convert_t(shifted(b, -by), shifted(a, -j))


    def lanes_of(z_of):
        return pl.ds(pl.multiple_of(z_of * MZ, MZ), MZ)

    def half(core):
        return pl.ds(pl.multiple_of(core * (MZ // 2), MZ // 2), MZ // 2)

    last = len(CHUNKS)
    z_first = [k < last - A_FIRST for k in range(last)]

    def convert_v(k):
        size = CHUNKS[k]
        n = SIDE * size
        wait_received(vbuf.at[pl.ds(0, 3), pl.ds(starts[k], size)], v_recv.at[k])

        @pl.loop(0, SIDE)
        def _(s):
            high, low = pl.ds(pl.multiple_of(s * size, size), size), pl.ds(pl.multiple_of(n + s * size, size), size)
            vhl[high, :], vhl[low, :] = split(vbuf[s, pl.ds(starts[k], size), :])

    def multiply(k, m):
        n = SIDE * CHUNKS[k]
        both = dot_nt(vhl[pl.ds(0, 2 * n), :], thi[m, :])
        ct[k, pl.ds(0, n), m] = both[:n] + both[n:] + dot_nt(vhl[pl.ds(0, n), :], tlo[m, :])

    def z_copy(k, j):
        n = pl.ds(0, SIDE * CHUNKS[k])
        return remote(ct.at[k, n, lanes_of(shifted(z, j))], zbuf.at[k, j - 1, n], z_send.at[k], z_recv.at[k], along_z(j))

    def early_tiles():
        @pl.loop(0, SIDE)
        def _(i):
            j = i + i // 2 - 2 * (i // 3)
            wait_received(tbuf.at[0], f_recv.at[j])
            convert_t(shifted(b, 2), shifted(a, -j))
            z_of = shifted(y, -j)
            multiply(0, lanes_of(z_of))
            by = shifted(z_of, -z)

            @pl.when(by != 0)
            def _():
                z_copy(0, by).start()

        wait_sent(zbuf.at[0, :, pl.ds(0, SIDE * CHUNKS[0])], z_send.at[0])

    def a_first_copy(k, j, i):
        size, f = CHUNKS[k], k - last + A_FIRST
        m = lanes_of(shifted(z, j))
        part = pl.ds(pl.multiple_of(shifted(a, i) * size, size), size)
        return remote(ct.at[k, part, m], afirst.at[f, i - 1, pl.ds(0, size), m], b_send.at[f],
                      b_recv.at[SIDE * f + j], along_a(i))

    def half_tiles(k, h):
        size = CHUNKS[k]
        n = SIDE * size
        lanes = pl.ds(h * (KQ // 2), KQ // 2)
        wait_received(vbuf.at[pl.ds(0, 3), pl.ds(starts[k], size), lanes], v_recv.at[k + h])

        @pl.loop(0, SIDE)
        def _(s):
            high, low = pl.ds(pl.multiple_of(s * size, size), size), pl.ds(pl.multiple_of(n + s * size, size), size)
            vhl[high, lanes], vhl[low, lanes] = split(vbuf[s, pl.ds(starts[k], size), lanes])

        @pl.loop(0, SIDE)
        def _(step):
            j = (step + 1) % SIDE
            m = lanes_of(shifted(z, j))
            both = dot_nt(vhl[pl.ds(0, 2 * n), lanes], thi[m, lanes])
            value = both[:n] + both[n:] + dot_nt(vhl[pl.ds(0, n), lanes], tlo[m, lanes])
            if h == 0:
                ct[k, pl.ds(0, n), m] = value
            else:
                ct[k, pl.ds(0, n), m] += value
                for i in (2, 1, 3):
                    a_first_copy(k, j, i).start()

    def all_tiles(k):
        if k == last - 1:
            half_tiles(k, 0)
            half_tiles(k, 1)
            wait_sent(afirst.at[k - last + A_FIRST, :, pl.ds(0, CHUNKS[k])], b_send.at[k - last + A_FIRST])
            return
        convert_v(k)

        n = SIDE * CHUNKS[k]

        def opposite_half(w):
            part = ct.at[k, pl.ds(w * n // 2, n // 2), lanes_of(shifted(z, 2))]
            return remote(part, zh.at[k, w, pl.ds(0, n // 2)], h_send.at[k], h_recv.at[k], along_z(1 - 2 * w))

        @pl.loop(0, SIDE)
        def _(step):
            j = (step + 2) % SIDE if z_first[k] else (step + 1) % SIDE
            multiply(k, lanes_of(shifted(z, j)))
            if k == last - A_FIRST:
                @pl.when(step == 1)
                def _():
                    onward_z(k - 1)
            if z_first[k]:
                @pl.when(step == 0)
                def _():
                    for w in (0, 1):
                        opposite_half(w).start()
            else:
                for i in (2, 1, 3):
                    a_first_copy(k, j, i).start()

        if z_first[k]:
            wait_sent(zh.at[k, :, pl.ds(0, n // 2)], h_send.at[k])
            wait_sent(zbuf.at[k, pl.ds(0, 2), pl.ds(0, n)], z_send.at[k])
        else:
            f = k - last + A_FIRST
            wait_sent(afirst.at[f, :, pl.ds(0, CHUNKS[k])], b_send.at[f])

    def onward_z(k):
        n = SIDE * CHUNKS[k]
        wait_received(zh.at[k, :, pl.ds(0, n // 2)], h_recv.at[k])
        for w in (0, 1):
            m = lanes_of(shifted(z, 1 - 2 * w))
            rows = pl.ds(0, n)
            ct[k, pl.ds(w * n // 2, n // 2), m] += zh[k, w, pl.ds(0, n // 2), :]
            go(remote(ct.at[k, rows, m], zbuf.at[k, w, rows], z_send.at[k], z_recv.at[k], along_z(1 - 2 * w)))

    def reduce_first(k):
        size = CHUNKS[k]
        q = pl.ds(0, size)
        if z_first[k]:
            n = pl.ds(0, SIDE * size)
            pieces = 2 if k else 3
            wait_received(zbuf.at[k, pl.ds(0, pieces), n], z_recv.at[k])
            value = ct[k, n, lanes_of(z)]
            for at in range(pieces):
                value += zbuf[k, at, n, :]
            zs[k, n, :] = value
            for j in (2, 1, 3, 0):
                part = pl.ds(pl.multiple_of(shifted(a, j) * size, size), size)
                for core in (0, 1):
                    if j or core:
                        to = device(shifted(a, j), b, z, (c + core) % 2)
                        go(remote(zs.at[k, part, half((c + core) % 2)], abuf.at[k, 2 * j + core - 1, q], a_send.at[k], a_recv.at[k], to))
            wait_sent(abuf.at[k, :, q], a_send.at[k])
        else:
            f = k - last + A_FIRST
            own = pl.ds(pl.multiple_of(a * size, size), size)
            for j in (1, 2, 3, 0):
                m = lanes_of(shifted(z, j))
                wait_received(afirst.at[f, :, q, m], b_recv.at[SIDE * f + j])
                ct[k, own, m] = ct[k, own, m] + afirst[f, 0, q, m] + afirst[f, 1, q, m] + afirst[f, 2, q, m]
                for core in (0, 1):
                    if j or core:
                        at = 2 * j + core - 1
                        part = pl.ds(pl.multiple_of(shifted(z, j) * MZ + ((c + core) % 2) * (MZ // 2), MZ // 2), MZ // 2)
                        go(remote(ct.at[k, own, part], zdirect.at[f, at, q], d_send.at[f], d_recv.at[f],
                                  device(a, b, shifted(z, j), (c + core) % 2)))
            wait_sent(zdirect.at[f, :, q], d_send.at[f])

    def write(k, value):
        rows = pl.ds(starts[k], CHUNKS[k])
        o_ref[rows, :] = value

    def finish(k):
        size = CHUNKS[k]
        own = pl.ds(pl.multiple_of(a * size, size), size)
        q = pl.ds(0, size)
        if z_first[k]:
            parts, at_k, recv, value = abuf, k, a_recv, zs[k, own, half(c)]
        else:
            f = k - last + A_FIRST
            parts, at_k, recv = zdirect, f, d_recv
            value = ct[k, own, pl.ds(pl.multiple_of(z * MZ + c * (MZ // 2), MZ // 2), MZ // 2)]
        wait_received(parts.at[at_k, :, q], recv.at[at_k])
        for at in range(7):
            value += parts[at_k, at, q, :]
        o_ref[pl.ds(starts[k], size), :] = value

    gather(0, t_ref.at[:, columns(a)])
    send_v(0)
    t_copies[1].wait_recv()
    gather(1, tbuf.at[slot(b, shifted(a, -1))])
    t_copies[3].wait_recv()
    gather(3, tbuf.at[slot(b, shifted(a, -3))])
    forward(0)
    t_copies[2].wait_recv()
    gather(2, tbuf.at[slot(b, shifted(a, -2))])
    t_own.wait()
    v_own.wait()
    pl.loop(0, SIDE)(lambda j: convert_t(b, shifted(a, -j)))
    forward(1)
    forward(3)
    forward(2)
    pl.loop(0, SIDE)(convert_sides)
    convert_v(0)
    send_v(1)
    early_tiles()

    for k in range(1, last):
        for later in range(2 if k == 1 else k + 2, min(k + 3, last)):
            if later < last - 1:
                send_v(later)
        if k == 1:
            send_v_half(0)
        if k == last - 2 - LATE:
            send_v_half(1)
        all_tiles(k)
        if k < last - A_FIRST and not (DELAY and k == last - A_FIRST - 1):
            onward_z(k)
    for k in [0, 1, last - 2, last - 3, last - 1]:
        reduce_first(k)
    for k in range(last):
        finish(k)
    for copy in sent:
        copy.wait_send()


def local(amplitudes, integrals):
    steps, most = len(CHUNKS), max(CHUNKS)
    bf16, f32 = jnp.bfloat16, jnp.float32
    dma = pltpu.SemaphoreType.DMA
    return pl.pallas_call(
        kernel,
        out_shape=pltpu.VMEM((VROWS, MZ // 2), f32),
        in_specs=[pl.BlockSpec(memory_space=pl.ANY)] * 2,
        out_specs=pl.BlockSpec(memory_space=pltpu.VMEM),
        scratch_shapes=[
            pltpu.VMEM((SIDE * SIDE, TROWS, KQ), f32),
            pltpu.VMEM((SIDE, VROWS, KQ), f32),
            pltpu.VMEM((SIDE * SIDE * TROWS, KQ), bf16),
            pltpu.VMEM((SIDE * SIDE * TROWS, KQ), bf16),
            pltpu.VMEM((2 * SIDE * most, KQ), bf16),
            pltpu.VMEM((steps, SIDE * most, SIDE * MZ), f32),
            pltpu.VMEM((steps, 2, SIDE * most // 2, MZ), f32),
            pltpu.VMEM((steps, SIDE - 1, SIDE * most, MZ), f32),
            pltpu.VMEM((steps, SIDE * most, MZ), f32),
            pltpu.VMEM((steps, 7, most, MZ // 2), f32),
            pltpu.VMEM((A_FIRST, SIDE - 1, most, SIDE * MZ), f32),
            pltpu.VMEM((A_FIRST, 7, most, MZ // 2), f32),
            dma(()), dma((SIDE - 1,)),
            dma(()), dma((2 * SIDE,)),
            dma(()), dma((SIDE,)),
            dma(()), dma((steps + 1,)),
            dma((steps - A_FIRST,)), dma((steps - A_FIRST,)),
            dma((steps - A_FIRST,)), dma((steps - A_FIRST,)),
            dma((A_FIRST,)), dma((A_FIRST,)),
            dma((A_FIRST,)), dma((SIDE * A_FIRST,)),
            dma((steps - A_FIRST,)), dma((steps - A_FIRST,)),
            dma((2,)),
        ],
        compiler_params=pltpu.CompilerParams(collective_id=0, has_side_effects=True, vmem_limit_bytes=VMEM_BYTES),
        cost_estimate=pl.CostEstimate(flops=3 * 2 * 1024 * 1024 * KQ, bytes_accessed=10 << 20, transcendentals=0),
    )(amplitudes, integrals).T


def solution(mesh):
    in_specs = (P("ab", "ij"), P("ab", "ij"))
    out_specs = P("ij", "ab")
    return jax.shard_map(local, mesh=mesh, in_specs=in_specs, out_specs=out_specs, check_vma=False)
```
